32 devices in a mesh: gx: 8 (over y, x, core), gz: 4 (over z).
Axes of the slice: x: 2, y: 2, z: 4, core: 2. Of those that a mesh axis runs over, the one named last changes fastest.
Arguments:
- field: bfloat16 [512, 16, 512], P('gx', None, 'gz'), may hold values from -6 to 6
- even_vectors: bfloat16 [256, 256], P('gx', 'gz'), may hold values from -0.375 to 0.375
- odd_vectors: bfloat16 [256, 256], P('gx', 'gz'), may hold values from -0.375 to 0.375
Outputs:
- even_modes: float32 [256, 16, 512], P('gx', None, 'gz')
- odd_modes: float32 [256, 16, 512], P('gx', None, 'gz')
The draws below stay inside these ranges and needn't reach their ends.
All inputs are finite; a program needn't handle non-finite values.
Results may differ from the reference program's by a relative error of at most 0.0031.
Values may be sent and summed in bfloat16 or wider, within the bound.
No kernel may reach another device: no remote copies, remote signals or barrier semaphores. Data moves between devices by JAX's collectives and lax.ppermute only.
A program may use at most 64 MiB of HBM per device.

```python
import jax
import jax.numpy as jnp

WY = 16
NX = 512
HALF = 256
NZ = 512


def shard_levels(key, dims, cuts, smallest, largest):
    level = 1.0
    for axis_at, parts in cuts:
        heights = jax.random.uniform(jax.random.fold_in(jax.random.fold_in(key, 6), axis_at), (parts,), jnp.float32, smallest / len(cuts), largest / len(cuts))
        level = level * jnp.repeat(jnp.exp(heights), dims[axis_at] // parts).reshape((-1,) + (1,) * (len(dims) - 1 - axis_at))
    return level


def bell_draw(rng, extent, scale, bound, pieces=(), held_as=jnp.bfloat16):
    gain = shard_levels(rng, extent, pieces, -0.22, 0.18) if pieces else 1.0
    values = jax.random.normal(rng, extent, jnp.float32) * scale * gain
    return jnp.minimum(jnp.maximum(values, -bound), bound).astype(held_as)


def setup_inputs(seed: int = 0) -> dict:
    keys = jax.random.split(jax.random.key(seed), 4)
    field = bell_draw(keys[0], (NX, WY, NZ), 1.0, 6.0, ((0, 8), (2, 4)))
    even_vectors = bell_draw(keys[1], (HALF, HALF), HALF ** -0.5, 0.375, ((0, 8), (1, 4)))
    odd_vectors = bell_draw(keys[2], (HALF, HALF), HALF ** -0.5, 0.375, ((0, 8), (1, 4)))
    return {"field": field, "even_vectors": even_vectors, "odd_vectors": odd_vectors}


def reference(field, even_vectors, odd_vectors):
    flat = field.reshape(NX, WY * NZ)
    lower = flat[:HALF].astype(jnp.float32)
    upper = flat[HALF:][::-1].astype(jnp.float32)
    even_part = (lower + upper).astype(jnp.bfloat16)
    odd_part = (lower - upper).astype(jnp.bfloat16)
    even_modes = jnp.dot(even_vectors, even_part, preferred_element_type=jnp.float32)
    odd_modes = jnp.dot(odd_vectors, odd_part, preferred_element_type=jnp.float32)
    return even_modes.reshape(HALF, WY, NZ), odd_modes.reshape(HALF, WY, NZ)
```

```python
import functools

import jax
import jax.numpy as jnp
from jax import lax
from jax.experimental import pallas as pl
from jax.experimental.pallas import tpu as pltpu
from jax.sharding import PartitionSpec as P


def pair_sums(first, second, upper, even_lines, odd_lines, rows, planes, depth, at):
    def spread(even_ref, odd_ref):
        for j in range(rows):
            here = pl.ds(j * planes, planes)
            there = pl.ds((rows - 1 - j) * planes, planes)
            low = jnp.where(upper, second[here, :], first[here, :]).astype(jnp.float32)
            high = jnp.where(upper, first[there, :], second[there, :]).astype(
                jnp.float32
            )
            even_ref[here, :] = low + high
            odd_ref[here, :] = low - high
        for y in range(planes):
            line = pl.ds(y, rows, stride=planes)
            columns = pl.ds(y * depth, depth)
            even_lines[at, columns] = even_ref[line, :].astype(jnp.bfloat16)
            odd_lines[at, columns] = odd_ref[line, :].astype(jnp.bfloat16)

    pl.run_scoped(
        spread,
        pltpu.VMEM((rows * planes, depth), jnp.float32),
        pltpu.VMEM((rows * planes, depth), jnp.float32),
    )


def transform_kernel(pairs, rows, planes, depth, has_sum, places, vectors, *refs):
    blocks = refs[: 2 * pairs]
    refs = refs[2 * pairs :]
    if has_sum:
        sum_own, sum_other = refs[:2]
        refs = refs[2:]
    own, other, even_lines, odd_lines = refs
    core = places[0]
    for p in range(pairs):
        pair_sums(
            blocks[2 * p],
            blocks[2 * p + 1],
            places[1 + 2 * p] > 0,
            even_lines,
            odd_lines,
            rows,
            planes,
            depth,
            pl.ds(p * rows, rows),
        )
    for result, before, which in (
        (own, sum_own if has_sum else None, core),
        (other, sum_other if has_sum else None, 1 - core),
    ):
        for parity, lines in enumerate((even_lines, odd_lines)):
            total = before[parity] if has_sum else None
            for p in range(pairs):
                block = vectors[places[2 + 2 * p], which, parity]
                part = jnp.dot(
                    block,
                    lines[pl.ds(p * rows, rows), :],
                    preferred_element_type=jnp.float32,
                )
                total = part if total is None else total + part
            result[parity] = total


def transform(places, vectors, blocks, sums, planes):
    pairs = len(blocks) // 2
    lines, depth = blocks[0].shape
    rows = lines // planes
    modes = vectors.shape[3]
    shape = jax.ShapeDtypeStruct((2, modes, planes * depth), jnp.float32)
    vmem = pl.BlockSpec(memory_space=pltpu.VMEM)
    return pl.pallas_call(
        functools.partial(
            transform_kernel, pairs, rows, planes, depth, bool(sums)
        ),
        out_shape=(shape, shape),
        in_specs=[pl.BlockSpec(memory_space=pltpu.SMEM)]
        + [vmem] * (1 + len(blocks) + len(sums)),
        out_specs=(vmem, vmem),
        scratch_shapes=[
            pltpu.VMEM((pairs * rows, planes * depth), jnp.bfloat16),
            pltpu.VMEM((pairs * rows, planes * depth), jnp.bfloat16),
        ],
        compiler_params=pltpu.CompilerParams(vmem_limit_bytes=48 * 1024 * 1024),
        name="transform",
    )(places, vectors, *blocks, *sums)


def finish_kernel(planes, depth, own, received, even_out, odd_out):
    modes = own.shape[1]
    for parity, out in enumerate((even_out, odd_out)):
        for y in range(planes):
            columns = pl.ds(y * depth, depth)
            out[pl.ds(y, modes, stride=planes), :] = (
                own[parity, :, columns] + received[parity, :, columns]
            )


def finish(own, received, planes, depth):
    modes = own.shape[1]
    shape = jax.ShapeDtypeStruct((modes * planes, depth), jnp.float32)
    vmem = pl.BlockSpec(memory_space=pltpu.VMEM)
    return pl.pallas_call(
        functools.partial(finish_kernel, planes, depth),
        out_shape=(shape, shape),
        in_specs=[vmem, vmem],
        out_specs=(vmem, vmem),
        compiler_params=pltpu.CompilerParams(vmem_limit_bytes=48 * 1024 * 1024),
        name="finish",
    )(own, received)


def local(field, even_vectors, odd_vectors):
    count = lax.axis_size("gx")
    slices = lax.axis_size("gz")
    me = lax.axis_index("gx")
    z = lax.axis_index("gz")
    rows, planes, depth = field.shape
    modes = even_vectors.shape[0]
    top = count // 2
    masks = [1 << b for b in range(1, count.bit_length() - 2)] + [top | 1]

    def in_first(g):
        return (g & 1) == (g // top)

    def swap(value, mask):
        return lax.ppermute(value, "gx", [(g, g ^ mask) for g in range(count)])

    def swap_two(value, first, second):
        return lax.ppermute(
            value,
            "gx",
            [(g, g ^ (first if in_first(g) else second)) for g in range(count)],
        )

    held = [field]
    for a, b in zip(masks, reversed(masks)):
        held = held + [swap_two(block, a, b) for block in held]
    packed = jnp.stack((even_vectors, odd_vectors))[None]
    step = 1
    while step < slices:
        moved = lax.ppermute(packed, "gz", [(i, i ^ step) for i in range(slices)])
        packed = jnp.concatenate((packed, moved))
        step *= 2
    partner = swap(packed, 1)
    core = me & 1
    vectors = jnp.where(
        core == 0, jnp.stack((packed, partner), 1), jnp.stack((partner, packed), 1)
    )

    flat = [block.reshape(rows * planes, depth) for block in held]
    first_set = (me & 1) == (me // top)

    def places(ks):
        out = [core]
        for k in ks:
            first = second = 0
            for s, (a, b) in enumerate(zip(masks, reversed(masks))):
                if k >> s & 1:
                    first, second = first ^ a, second ^ b
            at = me ^ jnp.where(first_set, first, second)
            upper = at >= top
            block = jnp.where(upper, count - 1 - at, at)
            out += [upper.astype(jnp.int32), z ^ block]
        return jnp.stack(out).astype(jnp.int32)

    last = len(held) - 1
    early = range(1, len(held) // 2)
    sums = transform(
        places(early),
        vectors,
        [flat[i] for k in early for i in (k, last - k)],
        (),
        planes,
    )
    own, other = transform(places([0]), vectors, [flat[0], flat[last]], sums, planes)
    received = swap(other, 1)
    even, odd = finish(own, received, planes, depth)
    return even.reshape(modes, planes, depth), odd.reshape(modes, planes, depth)


def solution(mesh):
    placed = (P("gx", None, "gz"), P("gx", "gz"), P("gx", "gz"))
    return jax.shard_map(
        local,
        mesh=mesh,
        in_specs=placed,
        out_specs=(P("gx", None, "gz"), P("gx", None, "gz")),
        check_vma=False,
    )
```

```python
import functools

import jax
import jax.numpy as jnp
from jax import lax
from jax.experimental import pallas as pl
from jax.experimental.pallas import tpu as pltpu
from jax.sharding import PartitionSpec as P

PARAMS = pltpu.CompilerParams(vmem_limit_bytes=48 * 1024 * 1024)
CHUNK = 16


class Block:
    def __init__(self, value, even, odd):
        self.value, self.even, self.odd = value, even, odd

    def place(self, count):
        me = lax.axis_index("gx")
        at = me ^ jnp.where((me & 1) == 0, self.even, self.odd)
        upper = (at >= count // 2).astype(jnp.int32)
        block = jnp.where(upper == 1, count - 1 - at, at)
        return upper, lax.axis_index("gz") ^ block


def send(block, even, odd, count):
    pairs = [(g, g ^ (odd if g & 1 else even)) for g in range(count)]
    if even & 1:
        offsets = odd ^ block.odd, even ^ block.even
    else:
        offsets = even ^ block.even, odd ^ block.odd
    return Block(lax.ppermute(block.value, "gx", pairs), *offsets)


def parity_lines(first, second, upper, planes, even, odd, start):
    lines, depth = first.shape
    rows = lines // planes

    def spread(low, high):
        for j in range(0, rows, CHUNK):
            evens, odds = [], []
            for i in range(j, j + CHUNK):
                a = low[pl.ds(i * planes, planes), :].astype(jnp.float32)
                b = high[pl.ds((rows - 1 - i) * planes, planes), :].astype(jnp.float32)
                evens.append((a + b).astype(jnp.bfloat16))
                odds.append((a - b).astype(jnp.bfloat16))
            for part, ref in ((evens, even), (odds, odd)):
                part = jnp.swapaxes(jnp.stack(part), 0, 1)
                for y in range(planes):
                    ref[pl.ds(start + j, CHUNK), pl.ds(y * depth, depth)] = part[y]

    @pl.when(upper == 0)
    def _():
        spread(first, second)

    @pl.when(upper != 0)
    def _():
        spread(second, first)


def prepare_kernel(place, planes, first, second, even, odd):
    parity_lines(first, second, place()[0], planes, even, odd, 0)


def prepare(pair, count, planes):
    lines, depth = pair[0].value.shape
    shape = jax.ShapeDtypeStruct((lines // planes, planes * depth), jnp.bfloat16)
    vmem = pl.BlockSpec(memory_space=pltpu.VMEM)
    return pl.pallas_call(
        functools.partial(
            prepare_kernel, functools.partial(pair[0].place, count), planes
        ),
        out_shape=(shape, shape),
        in_specs=[vmem, vmem],
        out_specs=(vmem, vmem),
        compiler_params=PARAMS,
        name="prepare",
    )(pair[0].value, pair[1].value)


def finish_kernel(places, planes, vectors, first, second, *refs):
    even_out, odd_out, even_last, odd_last = refs[-4:]
    earlier = refs[:-4]
    depth = first.shape[1]
    modes = vectors.shape[2]
    spots = [place() for place in places]
    parity_lines(first, second, spots[-1][0], planes, even_last, odd_last, 0)
    for parity, (out, last) in enumerate(((even_out, even_last), (odd_out, odd_last))):
        matrix = jnp.concatenate([vectors[at, parity] for _, at in spots], axis=1)
        lines = jnp.concatenate(
            [ref[...] for ref in earlier[parity::2]] + [last[...]], axis=0
        )
        result = jnp.dot(matrix, lines, preferred_element_type=jnp.float32)
        for y in range(planes):
            out[pl.ds(y, modes, stride=planes), :] = result[
                :, y * depth : (y + 1) * depth
            ]


def finish(pairs, count, planes, vectors, earlier):
    lines, depth = pairs[-1][0].value.shape
    rows = lines // planes
    modes = vectors.shape[2]
    shape = jax.ShapeDtypeStruct((modes * planes, depth), jnp.float32)
    vmem = pl.BlockSpec(memory_space=pltpu.VMEM)
    places = [functools.partial(first.place, count) for first, _ in pairs]
    return pl.pallas_call(
        functools.partial(finish_kernel, places, planes),
        out_shape=(shape, shape),
        in_specs=[vmem] * (3 + len(earlier)),
        out_specs=(vmem, vmem),
        scratch_shapes=[pltpu.VMEM((rows, planes * depth), jnp.bfloat16)] * 2,
        compiler_params=PARAMS,
        name="finish",
    )(vectors, pairs[-1][0].value, pairs[-1][1].value, *earlier)


def local(field, even_vectors, odd_vectors):
    count = lax.axis_size("gx")
    slices = lax.axis_size("gz")
    rows, planes, depth = field.shape
    modes = even_vectors.shape[0]
    masks = [1 << b | 1 for b in range(1, count.bit_length() - 1)]

    def widen(vectors, step):
        pairs = [(i, i ^ step) for i in range(slices)]
        return jnp.concatenate((vectors, lax.ppermute(vectors, "gz", pairs)))

    vectors = jnp.stack((even_vectors, odd_vectors))[None]
    steps = [1 << b for b in range(slices.bit_length() - 1)]
    held = [Block(field.reshape(rows * planes, depth), 0, 0)]
    while masks:
        a, b = (masks + masks)[:2]
        crossed = len(masks) > 1
        near = [send(block, a, b, count) for block in held]
        far = [send(block, b, a, count) for block in held] if crossed else []
        if steps:
            vectors = widen(vectors, steps.pop(0))
            vectors, near[0].value = lax.optimization_barrier((vectors, near[0].value))
        across = [send(block, a, b, count) for block in near] if crossed else []
        held += near + far + across
        masks = masks[2:]
    for step in steps:
        vectors = widen(vectors, step)
    held[-1].value, vectors = lax.optimization_barrier((held[-1].value, vectors))
    both = held + [send(block, 1, 1, count) for block in held]

    pairs, left = [], list(range(len(both)))
    while left:
        i = left.pop(0)
        j = next(
            j
            for j in left
            if both[j].even == both[i].even ^ (count - 1)
            and both[j].odd == both[i].odd ^ (count - 1)
        )
        left.remove(j)
        pairs.append((j, i))
    pairs = [(both[i], both[j]) for j, i in sorted(pairs)]
    early = []
    for pair in pairs[:-1]:
        early += prepare(pair, count, planes)
    even, odd = finish(pairs, count, planes, vectors, early)
    return even.reshape(modes, planes, depth), odd.reshape(modes, planes, depth)


def solution(mesh):
    placed = (P("gx", None, "gz"), P("gx", "gz"), P("gx", "gz"))
    return jax.shard_map(
        local,
        mesh=mesh,
        in_specs=placed,
        out_specs=(P("gx", None, "gz"), P("gx", None, "gz")),
        check_vma=False,
    )
```

```python
import functools

import jax
import jax.numpy as jnp
from jax import lax
from jax.experimental import pallas as pl
from jax.experimental.pallas import tpu as pltpu
from jax.sharding import PartitionSpec as P

PARAMS = pltpu.CompilerParams(vmem_limit_bytes=48 * 1024 * 1024)
CHUNK = 16


class Block:
    def __init__(self, value, even, odd):
        self.value, self.even, self.odd = value, even, odd

    def place(self, count):
        me = lax.axis_index("gx")
        at = me ^ jnp.where((me & 1) == 0, self.even, self.odd)
        upper = (at >= count // 2).astype(jnp.int32)
        block = jnp.where(upper == 1, count - 1 - at, at)
        return upper, lax.axis_index("gz") ^ block


def send(block, even, odd, count):
    pairs = [(g, g ^ (odd if g & 1 else even)) for g in range(count)]
    if even & 1:
        offsets = odd ^ block.odd, even ^ block.even
    else:
        offsets = even ^ block.even, odd ^ block.odd
    return Block(lax.ppermute(block.value, "gx", pairs), *offsets)


def parity_lines(first, second, upper, planes, even, odd, start):
    lines, depth = first.shape
    rows = lines // planes

    def spread(low, high):
        for j in range(0, rows, CHUNK):
            evens, odds = [], []
            for i in range(j, j + CHUNK):
                a = low[pl.ds(i * planes, planes), :].astype(jnp.float32)
                b = high[pl.ds((rows - 1 - i) * planes, planes), :].astype(jnp.float32)
                evens.append((a + b).astype(jnp.bfloat16))
                odds.append((a - b).astype(jnp.bfloat16))
            for part, ref in ((evens, even), (odds, odd)):
                part = jnp.swapaxes(jnp.stack(part), 0, 1)
                for y in range(planes):
                    ref[pl.ds(start + j, CHUNK), pl.ds(y * depth, depth)] = part[y]

    @pl.when(upper == 0)
    def _():
        spread(first, second)

    @pl.when(upper != 0)
    def _():
        spread(second, first)


def prepare_kernel(place, planes, first, second, even, odd):
    parity_lines(first, second, place()[0], planes, even, odd, 0)


def prepare(pair, count, planes):
    lines, depth = pair[0].value.shape
    shape = jax.ShapeDtypeStruct((lines // planes, planes * depth), jnp.bfloat16)
    vmem = pl.BlockSpec(memory_space=pltpu.VMEM)
    return pl.pallas_call(
        functools.partial(
            prepare_kernel, functools.partial(pair[0].place, count), planes
        ),
        out_shape=(shape, shape),
        in_specs=[vmem, vmem],
        out_specs=(vmem, vmem),
        compiler_params=PARAMS,
        name="prepare",
    )(pair[0].value, pair[1].value)


def combine_kernel(places, planes, last, vectors, first, second, *refs):
    ready = 2 * (len(places) - 1)
    lines, sums, (*outs, even, odd) = refs[:ready], refs[ready], refs[ready + last :]
    depth = first.shape[1]
    modes = vectors.shape[2]
    spots = [place() for place in places]
    parity_lines(first, second, spots[-1][0], planes, even, odd, 0)
    for parity, fresh in enumerate((even, odd)):
        matrix = jnp.concatenate([vectors[at, parity] for _, at in spots], axis=1)
        parts = jnp.concatenate(
            [ref[...] for ref in lines[parity::2]] + [fresh[...]], axis=0
        )
        result = jnp.dot(matrix, parts, preferred_element_type=jnp.float32)
        if not last:
            outs[0][parity] = result
            continue
        result = result + sums[parity]
        for y in range(planes):
            outs[parity][pl.ds(y, modes, stride=planes), :] = result[
                :, y * depth : (y + 1) * depth
            ]


def combine(vectors, pair, count, planes, ready=(), sums=None):
    last = sums is not None
    first, second = (block.value for block in pair)
    lines, depth = first.shape
    rows = lines // planes
    modes = vectors.shape[2]
    if last:
        shape = [jax.ShapeDtypeStruct((modes * planes, depth), jnp.float32)] * 2
    else:
        shape = [jax.ShapeDtypeStruct((2, modes, planes * depth), jnp.float32)]
    operands = [vectors, first, second]
    for _, parts in ready:
        operands += parts
    if last:
        operands.append(sums)
    places = [functools.partial(block.place, count) for block, _ in ready]
    places.append(functools.partial(pair[0].place, count))
    vmem = pl.BlockSpec(memory_space=pltpu.VMEM)
    return pl.pallas_call(
        functools.partial(combine_kernel, places, planes, last),
        out_shape=shape,
        in_specs=[vmem] * len(operands),
        out_specs=[vmem] * len(shape),
        scratch_shapes=[pltpu.VMEM((rows, planes * depth), jnp.bfloat16)] * 2,
        compiler_params=PARAMS,
        name="finish" if last else "combine",
    )(*operands)


def local(field, even_vectors, odd_vectors):
    count = lax.axis_size("gx")
    slices = lax.axis_size("gz")
    rows, planes, depth = field.shape
    modes = even_vectors.shape[0]
    masks = [1 << b | 1 for b in range(1, count.bit_length() - 1)]

    def widen(vectors, step):
        pairs = [(i, i ^ step) for i in range(slices)]
        return jnp.concatenate((vectors, lax.ppermute(vectors, "gz", pairs)))

    def after(block, *values):
        value = lax.optimization_barrier((block.value, *values))[0]
        return Block(value, block.even, block.odd)

    vectors = jnp.stack((even_vectors, odd_vectors))[None]
    steps = [1 << b for b in range(slices.bit_length() - 1)]
    held = [Block(field.reshape(rows * planes, depth), 0, 0)]
    while masks:
        a, b = (masks + masks)[:2]
        crossed = len(masks) > 1
        near = [send(block, a, b, count) for block in held]
        far = [send(block, b, a, count) for block in held] if crossed else []
        if steps:
            vectors = widen(vectors, steps.pop(0))
            near[0] = after(near[0], vectors)
        across = [send(block, a, b, count) for block in near] if crossed else []
        held += near + far + across
        masks = masks[2:]
    for step in steps:
        vectors = widen(vectors, step)
    others = []
    for block in held[:-1]:
        block = after(block, *(other.value for other in others[:1]))
        others.append(send(block, 1, 1, count))
    others.append(send(after(held[-1], vectors), 1, 1, count))

    both = held[:-1] + others[:-1] + [held[-1], others[-1]]
    pairs, left = [], list(range(len(both)))
    while left:
        i = left.pop(0)
        j = next(
            j
            for j in left
            if both[j].even == both[i].even ^ (count - 1)
            and both[j].odd == both[i].odd ^ (count - 1)
        )
        left.remove(j)
        pairs.append((j, i))
    pairs = [(both[i], both[j]) for j, i in sorted(pairs)]
    ready = [(pair[0], prepare(pair, count, planes)) for pair in pairs[:-2]]
    (sums,) = combine(vectors, pairs[-2], count, planes, ready)
    even, odd = combine(vectors, pairs[-1], count, planes, sums=sums)
    return even.reshape(modes, planes, depth), odd.reshape(modes, planes, depth)


def solution(mesh):
    placed = (P("gx", None, "gz"), P("gx", "gz"), P("gx", "gz"))
    return jax.shard_map(
        local,
        mesh=mesh,
        in_specs=placed,
        out_specs=(P("gx", None, "gz"), P("gx", None, "gz")),
        check_vma=False,
    )
```

```python
import functools

import jax
import jax.numpy as jnp
from jax import lax
from jax.experimental import pallas as pl
from jax.experimental.pallas import tpu as pltpu
from jax.sharding import PartitionSpec as P

PARAMS = pltpu.CompilerParams(vmem_limit_bytes=48 * 1024 * 1024)
CHUNK = 16


class Block:
    def __init__(self, value, even, odd):
        self.value, self.even, self.odd = value, even, odd

    def place(self, count):
        me = lax.axis_index("gx")
        bits = sum((me >> b) & 1 for b in range(count.bit_length() - 1))
        at = me ^ jnp.where((bits & 1) == 0, self.even, self.odd)
        upper = (at >= count // 2).astype(jnp.int32)
        block = jnp.where(upper == 1, count - 1 - at, at)
        return upper, lax.axis_index("gz") ^ block


def send(block, even, odd, count):
    pairs = [(g, g ^ (odd if g.bit_count() & 1 else even)) for g in range(count)]
    if even.bit_count() & 1:
        offsets = even ^ block.odd, odd ^ block.even
    else:
        offsets = even ^ block.even, odd ^ block.odd
    return Block(lax.ppermute(block.value, "gx", pairs), *offsets)


def parity_lines(first, second, upper, planes, even, odd, start):
    lines, depth = first.shape
    rows = lines // planes

    def spread(low, high):
        for j in range(0, rows, CHUNK):
            evens, odds = [], []
            for i in range(j, j + CHUNK):
                a = low[pl.ds(i * planes, planes), :].astype(jnp.float32)
                b = high[pl.ds((rows - 1 - i) * planes, planes), :].astype(jnp.float32)
                evens.append((a + b).astype(jnp.bfloat16))
                odds.append((a - b).astype(jnp.bfloat16))
            for part, ref in ((evens, even), (odds, odd)):
                part = jnp.swapaxes(jnp.stack(part), 0, 1)
                for y in range(planes):
                    ref[pl.ds(start + j, CHUNK), pl.ds(y * depth, depth)] = part[y]

    @pl.when(upper == 0)
    def _():
        spread(first, second)

    @pl.when(upper != 0)
    def _():
        spread(second, first)


def prepare_kernel(place, planes, first, second, even, odd):
    parity_lines(first, second, place()[0], planes, even, odd, 0)


def prepare(pair, count, planes):
    lines, depth = pair[0].value.shape
    shape = jax.ShapeDtypeStruct((lines // planes, planes * depth), jnp.bfloat16)
    vmem = pl.BlockSpec(memory_space=pltpu.VMEM)
    return pl.pallas_call(
        functools.partial(
            prepare_kernel, functools.partial(pair[0].place, count), planes
        ),
        out_shape=(shape, shape),
        in_specs=[vmem, vmem],
        out_specs=(vmem, vmem),
        compiler_params=PARAMS,
        name="prepare",
    )(pair[0].value, pair[1].value)


def combine_kernel(places, planes, last, vectors, first, second, *refs):
    ready = 2 * (len(places) - 1)
    lines, sums, (*outs, even, odd) = refs[:ready], refs[ready], refs[ready + last :]
    depth = first.shape[1]
    modes = vectors.shape[2]
    spots = [place() for place in places]
    parity_lines(first, second, spots[-1][0], planes, even, odd, 0)
    for parity, fresh in enumerate((even, odd)):
        matrix = jnp.concatenate([vectors[at, parity] for _, at in spots], axis=1)
        parts = jnp.concatenate(
            [ref[...] for ref in lines[parity::2]] + [fresh[...]], axis=0
        )
        result = jnp.dot(matrix, parts, preferred_element_type=jnp.float32)
        if not last:
            outs[0][parity] = result
            continue
        result = result + sums[parity]
        for y in range(planes):
            outs[parity][pl.ds(y, modes, stride=planes), :] = result[
                :, y * depth : (y + 1) * depth
            ]


def combine(vectors, pair, count, planes, ready=(), sums=None):
    last = sums is not None
    first, second = (block.value for block in pair)
    lines, depth = first.shape
    rows = lines // planes
    modes = vectors.shape[2]
    if last:
        shape = [jax.ShapeDtypeStruct((modes * planes, depth), jnp.float32)] * 2
    else:
        shape = [jax.ShapeDtypeStruct((2, modes, planes * depth), jnp.float32)]
    operands = [vectors, first, second]
    for _, parts in ready:
        operands += parts
    if last:
        operands.append(sums)
    places = [functools.partial(block.place, count) for block, _ in ready]
    places.append(functools.partial(pair[0].place, count))
    vmem = pl.BlockSpec(memory_space=pltpu.VMEM)
    return pl.pallas_call(
        functools.partial(combine_kernel, places, planes, last),
        out_shape=shape,
        in_specs=[vmem] * len(operands),
        out_specs=[vmem] * len(shape),
        scratch_shapes=[pltpu.VMEM((rows, planes * depth), jnp.bfloat16)] * 2,
        compiler_params=PARAMS,
        name="finish" if last else "combine",
    )(*operands)


def local(field, even_vectors, odd_vectors):
    count = lax.axis_size("gx")
    slices = lax.axis_size("gz")
    rows, planes, depth = field.shape
    modes = even_vectors.shape[0]
    masks = [1 << b | 1 for b in range(1, count.bit_length() - 1)]

    def widen(vectors, step):
        pairs = [(i, i ^ step) for i in range(slices)]
        return jnp.concatenate((vectors, lax.ppermute(vectors, "gz", pairs)))

    def after(block, *values):
        value = lax.optimization_barrier((block.value, *values))[0]
        return Block(value, block.even, block.odd)

    vectors = jnp.stack((even_vectors, odd_vectors))[None]
    steps = [1 << b for b in range(slices.bit_length() - 1)]
    held = [Block(field.reshape(rows * planes, depth), 0, 0)]
    while masks:
        a, b = (masks + masks)[:2]
        crossed = len(masks) > 1
        near = [send(block, a, b, count) for block in held]
        far = [send(block, b, a, count) for block in held] if crossed else []
        if steps:
            vectors = widen(vectors, steps.pop(0))
            near[0] = after(near[0], vectors)
        across = [send(block, b, a, count) for block in near] if crossed else []
        held += near + far + across
        masks = masks[2:]
    for step in steps:
        vectors = widen(vectors, step)
    others = []
    for block in held[:-1]:
        block = after(block, *(other.value for other in others[:1]))
        others.append(send(block, 1, 1, count))
    others.append(send(after(held[-1], vectors), 1, 1, count))

    both = held[:-1] + others[:-1] + [held[-1], others[-1]]
    pairs, left = [], list(range(len(both)))
    while left:
        i = left.pop(0)
        j = next(
            j
            for j in left
            if both[j].even == both[i].even ^ (count - 1)
            and both[j].odd == both[i].odd ^ (count - 1)
        )
        left.remove(j)
        pairs.append((j, i))
    pairs = [(both[i], both[j]) for j, i in sorted(pairs)]
    ready = [(pair[0], prepare(pair, count, planes)) for pair in pairs[:-2]]
    (sums,) = combine(vectors, pairs[-2], count, planes, ready)
    even, odd = combine(vectors, pairs[-1], count, planes, sums=sums)
    return even.reshape(modes, planes, depth), odd.reshape(modes, planes, depth)


def solution(mesh):
    placed = (P("gx", None, "gz"), P("gx", "gz"), P("gx", "gz"))
    return jax.shard_map(
        local,
        mesh=mesh,
        in_specs=placed,
        out_specs=(P("gx", None, "gz"), P("gx", None, "gz")),
        check_vma=False,
    )
```

```python
import functools

import jax
import jax.numpy as jnp
from jax import lax
from jax.experimental import pallas as pl
from jax.experimental.pallas import tpu as pltpu
from jax.sharding import PartitionSpec as P

PARAMS = pltpu.CompilerParams(vmem_limit_bytes=48 * 1024 * 1024)
CHUNK = 16


class Block:
    def __init__(self, value, even, odd):
        self.value, self.even, self.odd = value, even, odd

    def place(self, count):
        me = lax.axis_index("gx")
        bits = sum((me >> b) & 1 for b in range(count.bit_length() - 1))
        at = me ^ jnp.where((bits & 1) == 0, self.even, self.odd)
        upper = (at >= count // 2).astype(jnp.int32)
        block = jnp.where(upper == 1, count - 1 - at, at)
        return upper, lax.axis_index("gz") ^ block


def send(block, even, odd, count):
    pairs = [(g, g ^ (odd if g.bit_count() & 1 else even)) for g in range(count)]
    if even.bit_count() & 1:
        offsets = even ^ block.odd, odd ^ block.even
    else:
        offsets = even ^ block.even, odd ^ block.odd
    return Block(lax.ppermute(block.value, "gx", pairs), *offsets)


def parity_lines(first, second, upper, planes, even, odd, start):
    lines, depth = first.shape
    rows = lines // planes

    def spread(low, high):
        for j in range(0, rows, CHUNK):
            evens, odds = [], []
            for i in range(j, j + CHUNK):
                a = low[pl.ds(i * planes, planes), :]
                b = high[pl.ds((rows - 1 - i) * planes, planes), :]
                evens.append(a + b)
                odds.append(a - b)
            for part, ref in ((evens, even), (odds, odd)):
                part = jnp.swapaxes(jnp.stack(part), 0, 1)
                for y in range(planes):
                    ref[pl.ds(start + j, CHUNK), pl.ds(y * depth, depth)] = part[y]

    @pl.when(upper == 0)
    def _():
        spread(first, second)

    @pl.when(upper != 0)
    def _():
        spread(second, first)


def prepare_kernel(place, planes, first, second, even, odd):
    parity_lines(first, second, place()[0], planes, even, odd, 0)


def prepare(pair, count, planes):
    lines, depth = pair[0].value.shape
    shape = jax.ShapeDtypeStruct((lines // planes, planes * depth), jnp.bfloat16)
    vmem = pl.BlockSpec(memory_space=pltpu.VMEM)
    return pl.pallas_call(
        functools.partial(
            prepare_kernel, functools.partial(pair[0].place, count), planes
        ),
        out_shape=(shape, shape),
        in_specs=[vmem, vmem],
        out_specs=(vmem, vmem),
        compiler_params=PARAMS,
        name="prepare",
    )(pair[0].value, pair[1].value)


def combine_kernel(places, planes, last, vectors, first, second, *refs):
    ready = 2 * (len(places) - 1)
    lines, sums, (*outs, even, odd) = refs[:ready], refs[ready], refs[ready + last :]
    depth = first.shape[1]
    modes = vectors.shape[2]
    spots = [place() for place in places]
    parity_lines(first, second, spots[-1][0], planes, even, odd, 0)
    for parity, fresh in enumerate((even, odd)):
        matrix = jnp.concatenate([vectors[at, parity] for _, at in spots], axis=1)
        parts = jnp.concatenate(
            [ref[...] for ref in lines[parity::2]] + [fresh[...]], axis=0
        )
        result = jnp.dot(matrix, parts, preferred_element_type=jnp.float32)
        if not last:
            outs[0][parity] = result
            continue
        result = result + sums[parity]
        for y in range(planes):
            outs[parity][pl.ds(y, modes, stride=planes), :] = result[
                :, y * depth : (y + 1) * depth
            ]


def combine(vectors, pair, count, planes, ready=(), sums=None):
    last = sums is not None
    first, second = (block.value for block in pair)
    lines, depth = first.shape
    rows = lines // planes
    modes = vectors.shape[2]
    if last:
        shape = [jax.ShapeDtypeStruct((modes * planes, depth), jnp.float32)] * 2
    else:
        shape = [jax.ShapeDtypeStruct((2, modes, planes * depth), jnp.float32)]
    operands = [vectors, first, second]
    for _, parts in ready:
        operands += parts
    if last:
        operands.append(sums)
    places = [functools.partial(block.place, count) for block, _ in ready]
    places.append(functools.partial(pair[0].place, count))
    vmem = pl.BlockSpec(memory_space=pltpu.VMEM)
    return pl.pallas_call(
        functools.partial(combine_kernel, places, planes, last),
        out_shape=shape,
        in_specs=[vmem] * len(operands),
        out_specs=[vmem] * len(shape),
        scratch_shapes=[pltpu.VMEM((rows, planes * depth), jnp.bfloat16)] * 2,
        compiler_params=PARAMS,
        name="finish" if last else "combine",
    )(*operands)


def local(field, even_vectors, odd_vectors):
    count = lax.axis_size("gx")
    slices = lax.axis_size("gz")
    rows, planes, depth = field.shape
    modes = even_vectors.shape[0]
    masks = [1 << b | 1 for b in range(1, count.bit_length() - 1)]

    def widen(vectors, step):
        pairs = [(i, i ^ step) for i in range(slices)]
        return jnp.concatenate((vectors, lax.ppermute(vectors, "gz", pairs)))

    def after(block, *values):
        value = lax.optimization_barrier((block.value, *values))[0]
        return Block(value, block.even, block.odd)

    vectors = jnp.stack((even_vectors, odd_vectors))[None]
    steps = [1 << b for b in range(slices.bit_length() - 1)]
    held = [Block(field.reshape(rows * planes, depth), 0, 0)]
    while masks:
        a, b = (masks + masks)[:2]
        crossed = len(masks) > 1
        near = [send(block, a, b, count) for block in held]
        far = [send(block, b, a, count) for block in held] if crossed else []
        if steps:
            vectors = widen(vectors, steps.pop(0))
            near[0] = after(near[0], vectors)
        across = [send(block, b, a, count) for block in near] if crossed else []
        held += near + far + across
        masks = masks[2:]
    for step in steps:
        vectors = widen(vectors, step)
    others = []
    for block in held[:-1]:
        block = after(block, *(other.value for other in others[:1]))
        others.append(send(block, 1, 1, count))
    others.append(send(after(held[-1], vectors), 1, 1, count))

    both = held[:-1] + others[:-1] + [held[-1], others[-1]]
    pairs, left = [], list(range(len(both)))
    while left:
        i = left.pop(0)
        j = next(
            j
            for j in left
            if both[j].even == both[i].even ^ (count - 1)
            and both[j].odd == both[i].odd ^ (count - 1)
        )
        left.remove(j)
        pairs.append((j, i))
    pairs = [(both[i], both[j]) for j, i in sorted(pairs)]
    ready = [(pair[0], prepare(pair, count, planes)) for pair in pairs[:-2]]
    (sums,) = combine(vectors, pairs[-2], count, planes, ready)
    even, odd = combine(vectors, pairs[-1], count, planes, sums=sums)
    return even.reshape(modes, planes, depth), odd.reshape(modes, planes, depth)


def solution(mesh):
    placed = (P("gx", None, "gz"), P("gx", "gz"), P("gx", "gz"))
    return jax.shard_map(
        local,
        mesh=mesh,
        in_specs=placed,
        out_specs=(P("gx", None, "gz"), P("gx", None, "gz")),
        check_vma=False,
    )
```

```python
import functools

import jax
import jax.numpy as jnp
from jax import lax
from jax.experimental import pallas as pl
from jax.experimental.pallas import tpu as pltpu
from jax.sharding import PartitionSpec as P

PARAMS = pltpu.CompilerParams(vmem_limit_bytes=48 * 1024 * 1024)
CHUNK = 16


class Block:
    def __init__(self, value, even, odd):
        self.value, self.even, self.odd = value, even, odd

    def place(self, count):
        me = lax.axis_index("gx")
        bits = sum((me >> b) & 1 for b in range(count.bit_length() - 1))
        at = me ^ jnp.where((bits & 1) == 0, self.even, self.odd)
        upper = (at >= count // 2).astype(jnp.int32)
        block = jnp.where(upper == 1, count - 1 - at, at)
        return upper, lax.axis_index("gz") ^ block


def send(block, even, odd, count):
    pairs = [(g, g ^ (odd if g.bit_count() & 1 else even)) for g in range(count)]
    if even.bit_count() & 1:
        offsets = even ^ block.odd, odd ^ block.even
    else:
        offsets = even ^ block.even, odd ^ block.odd
    return Block(lax.ppermute(block.value, "gx", pairs), *offsets)


def parity_lines(first, second, planes, even, odd):
    lines, depth = first.shape
    rows = lines // planes
    for j in range(0, rows, CHUNK):
        evens, odds = [], []
        for i in range(j, j + CHUNK):
            a = first[pl.ds(i * planes, planes), :]
            b = second[pl.ds((rows - 1 - i) * planes, planes), :]
            evens.append(a + b)
            odds.append(a - b)
        for part, ref in ((evens, even), (odds, odd)):
            part = jnp.swapaxes(jnp.stack(part), 0, 1)
            for y in range(planes):
                ref[pl.ds(j, CHUNK), pl.ds(y * depth, depth)] = part[y]


def oriented(vectors, place):
    upper, at = place()
    modes, rows = vectors.shape[2:]
    row = lax.broadcasted_iota(jnp.int32, (rows, rows), 0)
    column = lax.broadcasted_iota(jnp.int32, (rows, rows), 1)
    chosen = jnp.where(upper == 1, rows - 1 - column, column)
    order = jnp.where(row == chosen, 1.0, 0.0).astype(vectors.dtype)
    sign = jnp.where(upper == 1, -1.0, 1.0)
    even, odd = (
        jnp.dot(vectors[at, parity], order, preferred_element_type=jnp.float32)
        for parity in (0, 1)
    )
    return even.astype(vectors.dtype), (odd * sign).astype(vectors.dtype)


def prepare_kernel(planes, first, second, even, odd):
    parity_lines(first, second, planes, even, odd)


def prepare(pair, planes):
    lines, depth = pair[0].value.shape
    shape = jax.ShapeDtypeStruct((lines // planes, planes * depth), jnp.bfloat16)
    vmem = pl.BlockSpec(memory_space=pltpu.VMEM)
    return pl.pallas_call(
        functools.partial(prepare_kernel, planes),
        out_shape=(shape, shape),
        in_specs=[vmem, vmem],
        out_specs=(vmem, vmem),
        compiler_params=PARAMS,
        name="prepare",
    )(pair[0].value, pair[1].value)


def combine_kernel(places, planes, vectors, first, second, *refs):
    *lines, sums, following, even, odd = refs
    matrices = [oriented(vectors, place) for place in places]
    for parity in (0, 1):
        following[parity] = matrices[-1][parity]
    parity_lines(first, second, planes, even, odd)
    for parity, fresh in enumerate((even, odd)):
        matrix = jnp.concatenate([both[parity] for both in matrices[:-1]], axis=1)
        parts = jnp.concatenate(
            [ref[...] for ref in lines[parity::2]] + [fresh[...]], axis=0
        )
        sums[parity] = jnp.dot(matrix, parts, preferred_element_type=jnp.float32)


def combine(vectors, ready, pair, following, count, planes):
    first, second = (block.value for block in pair)
    lines, depth = first.shape
    rows = lines // planes
    modes = vectors.shape[2]
    blocks = [block for block, _ in ready] + [pair[0], following]
    operands = [vectors, first, second] + [part for _, both in ready for part in both]
    vmem = pl.BlockSpec(memory_space=pltpu.VMEM)
    return pl.pallas_call(
        functools.partial(
            combine_kernel,
            [functools.partial(block.place, count) for block in blocks],
            planes,
        ),
        out_shape=(
            jax.ShapeDtypeStruct((2, modes, planes * depth), jnp.float32),
            jax.ShapeDtypeStruct((2, modes, rows), vectors.dtype),
        ),
        in_specs=[vmem] * len(operands),
        out_specs=(vmem, vmem),
        scratch_shapes=[pltpu.VMEM((rows, planes * depth), jnp.bfloat16)] * 2,
        compiler_params=PARAMS,
        name="combine",
    )(*operands)


def finish_kernel(planes, matrices, first, second, sums, *refs):
    *outs, even, odd = refs
    depth = first.shape[1]
    modes = matrices.shape[1]
    parity_lines(first, second, planes, even, odd)
    for parity, parts in enumerate((even, odd)):
        result = sums[parity] + jnp.dot(
            matrices[parity], parts[...], preferred_element_type=jnp.float32
        )
        for y in range(planes):
            outs[parity][pl.ds(y, modes, stride=planes), :] = result[
                :, y * depth : (y + 1) * depth
            ]


def finish(matrices, pair, sums, planes):
    first, second = (block.value for block in pair)
    lines, depth = first.shape
    modes = matrices.shape[1]
    shape = jax.ShapeDtypeStruct((modes * planes, depth), jnp.float32)
    vmem = pl.BlockSpec(memory_space=pltpu.VMEM)
    return pl.pallas_call(
        functools.partial(finish_kernel, planes),
        out_shape=(shape, shape),
        in_specs=[vmem] * 4,
        out_specs=(vmem, vmem),
        scratch_shapes=[pltpu.VMEM((lines // planes, planes * depth), jnp.bfloat16)]
        * 2,
        compiler_params=PARAMS,
        name="finish",
    )(matrices, first, second, sums)


def local(field, even_vectors, odd_vectors):
    count = lax.axis_size("gx")
    slices = lax.axis_size("gz")
    rows, planes, depth = field.shape
    modes = even_vectors.shape[0]
    masks = [1 << b | 1 for b in range(1, count.bit_length() - 1)]

    def widen(vectors, step):
        pairs = [(i, i ^ step) for i in range(slices)]
        return jnp.concatenate((vectors, lax.ppermute(vectors, "gz", pairs)))

    def after(block, *values):
        value = lax.optimization_barrier((block.value, *values))[0]
        return Block(value, block.even, block.odd)

    vectors = jnp.stack((even_vectors, odd_vectors))[None]
    steps = [1 << b for b in range(slices.bit_length() - 1)]
    held = [Block(field.reshape(rows * planes, depth), 0, 0)]
    while masks:
        a, b = (masks + masks)[:2]
        crossed = len(masks) > 1
        near = [send(block, a, b, count) for block in held]
        far = [send(block, b, a, count) for block in held] if crossed else []
        if steps:
            vectors = widen(vectors, steps.pop(0))
            near[0] = after(near[0], vectors)
        across = [send(block, b, a, count) for block in near] if crossed else []
        held += near + far + across
        masks = masks[2:]
    for step in steps:
        vectors = widen(vectors, step)
    others = []
    for block in held[:-1]:
        block = after(block, *(other.value for other in others[:1]))
        others.append(send(block, 1, 1, count))
    others.append(send(after(held[-1], vectors), 1, 1, count))

    both = held[:-1] + others[:-1] + [held[-1], others[-1]]
    pairs, left = [], list(range(len(both)))
    while left:
        i = left.pop(0)
        j = next(
            j
            for j in left
            if both[j].even == both[i].even ^ (count - 1)
            and both[j].odd == both[i].odd ^ (count - 1)
        )
        left.remove(j)
        pairs.append((j, i))
    pairs = [(both[i], both[j]) for j, i in sorted(pairs)]
    ready = [(pair[0], prepare(pair, planes)) for pair in pairs[:-2]]
    sums, matrices = combine(
        vectors, ready, pairs[-2], pairs[-1][0], count, planes
    )
    even, odd = finish(matrices, pairs[-1], sums, planes)
    return even.reshape(modes, planes, depth), odd.reshape(modes, planes, depth)


def solution(mesh):
    placed = (P("gx", None, "gz"), P("gx", "gz"), P("gx", "gz"))
    return jax.shard_map(
        local,
        mesh=mesh,
        in_specs=placed,
        out_specs=(P("gx", None, "gz"), P("gx", None, "gz")),
        check_vma=False,
    )
```

```python
import functools

import jax
import jax.numpy as jnp
from jax import lax
from jax.experimental import pallas as pl
from jax.experimental.pallas import tpu as pltpu
from jax.sharding import PartitionSpec as P

PARAMS = pltpu.CompilerParams(vmem_limit_bytes=48 * 1024 * 1024)
CHUNK = 16


class Block:
    def __init__(self, value, even, odd):
        self.value, self.even, self.odd = value, even, odd

    def place(self, count):
        me = lax.axis_index("gx")
        bits = sum((me >> b) & 1 for b in range(count.bit_length() - 1))
        at = me ^ jnp.where((bits & 1) == 0, self.even, self.odd)
        upper = (at >= count // 2).astype(jnp.int32)
        block = jnp.where(upper == 1, count - 1 - at, at)
        return upper, lax.axis_index("gz") ^ block


def send(block, even, odd, count):
    pairs = [(g, g ^ (odd if g.bit_count() & 1 else even)) for g in range(count)]
    if even.bit_count() & 1:
        offsets = even ^ block.odd, odd ^ block.even
    else:
        offsets = even ^ block.even, odd ^ block.odd
    return Block(lax.ppermute(block.value, "gx", pairs), *offsets)


def parity_lines(first, second, planes, even, odd):
    lines, depth = first.shape
    rows = lines // planes
    for j in range(0, rows, CHUNK):
        evens, odds = [], []
        for i in range(j, j + CHUNK):
            a = first[pl.ds(i * planes, planes), :]
            b = second[pl.ds((rows - 1 - i) * planes, planes), :]
            evens.append(a + b)
            odds.append(a - b)
        for part, ref in ((evens, even), (odds, odd)):
            part = jnp.swapaxes(jnp.stack(part), 0, 1)
            for y in range(planes):
                ref[pl.ds(j, CHUNK), pl.ds(y * depth, depth)] = part[y]


def oriented(vectors, place):
    upper, at = place()
    modes, rows = vectors.shape[2:]
    row = lax.broadcasted_iota(jnp.int32, (rows, rows), 0)
    column = lax.broadcasted_iota(jnp.int32, (rows, rows), 1)
    chosen = jnp.where(upper == 1, rows - 1 - column, column)
    order = jnp.where(row == chosen, 1.0, 0.0).astype(vectors.dtype)
    sign = jnp.where(upper == 1, -1.0, 1.0)
    even, odd = (
        jnp.dot(vectors[at, parity], order, preferred_element_type=jnp.float32)
        for parity in (0, 1)
    )
    return even.astype(vectors.dtype), (odd * sign).astype(vectors.dtype)


def prepare_kernel(planes, first, second, even, odd):
    parity_lines(first, second, planes, even, odd)


def prepare(pair, planes):
    lines, depth = pair[0].value.shape
    shape = jax.ShapeDtypeStruct((lines // planes, planes * depth), jnp.bfloat16)
    vmem = pl.BlockSpec(memory_space=pltpu.VMEM)
    return pl.pallas_call(
        functools.partial(prepare_kernel, planes),
        out_shape=(shape, shape),
        in_specs=[vmem, vmem],
        out_specs=(vmem, vmem),
        compiler_params=PARAMS,
        name="prepare",
    )(pair[0].value, pair[1].value)


def combine_kernel(places, planes, vectors, first, second, *refs):
    *lines, sums, following, even, odd = refs
    matrices = [oriented(vectors, place) for place in places]
    for parity in (0, 1):
        following[parity] = matrices[-1][parity]
    parity_lines(first, second, planes, even, odd)
    for parity, fresh in enumerate((even, odd)):
        matrix = jnp.concatenate([both[parity] for both in matrices[:-1]], axis=1)
        parts = jnp.concatenate(
            [ref[...] for ref in lines[parity::2]] + [fresh[...]], axis=0
        )
        sums[parity] = jnp.dot(matrix, parts, preferred_element_type=jnp.float32)


def combine(vectors, ready, pair, following, count, planes):
    first, second = (block.value for block in pair)
    lines, depth = first.shape
    rows = lines // planes
    modes = vectors.shape[2]
    blocks = [block for block, _ in ready] + [pair[0], following]
    operands = [vectors, first, second] + [part for _, both in ready for part in both]
    vmem = pl.BlockSpec(memory_space=pltpu.VMEM)
    return pl.pallas_call(
        functools.partial(
            combine_kernel,
            [functools.partial(block.place, count) for block in blocks],
            planes,
        ),
        out_shape=(
            jax.ShapeDtypeStruct((2, modes, planes * depth), jnp.float32),
            jax.ShapeDtypeStruct((2, modes, rows), vectors.dtype),
        ),
        in_specs=[vmem] * len(operands),
        out_specs=(vmem, vmem),
        scratch_shapes=[pltpu.VMEM((rows, planes * depth), jnp.bfloat16)] * 2,
        compiler_params=PARAMS,
        name="combine",
    )(*operands)


def finish_kernel(planes, matrices, lines, second, sums, *outs):
    depth = second.shape[1]
    modes = matrices.shape[1]
    here = lines[...]
    there = lines_of(second, planes, True)
    for parity, parts in enumerate((here + there, here - there)):
        result = sums[parity] + jnp.dot(
            matrices[parity], parts, preferred_element_type=jnp.float32
        )
        for y in range(planes):
            outs[parity][pl.ds(y, modes, stride=planes), :] = result[
                :, y * depth : (y + 1) * depth
            ]


def finish(matrices, lines, second, sums, planes):
    depth = second.value.shape[1]
    modes = matrices.shape[1]
    shape = jax.ShapeDtypeStruct((modes * planes, depth), jnp.float32)
    vmem = pl.BlockSpec(memory_space=pltpu.VMEM)
    return pl.pallas_call(
        functools.partial(finish_kernel, planes),
        out_shape=(shape, shape),
        in_specs=[vmem] * 4,
        out_specs=(vmem, vmem),
        compiler_params=PARAMS,
        name="finish",
    )(matrices, lines, second.value, sums)


def lines_of(block, planes, backwards):
    rows = block.shape[0] // planes
    order = range(rows - 1, -1, -1) if backwards else range(rows)
    lines = jnp.stack([block[pl.ds(i * planes, planes), :] for i in order])
    lines = jnp.swapaxes(lines, 0, 1)
    return jnp.concatenate([lines[y] for y in range(planes)], axis=1)


def bring_kernel(planes, source, lines):
    lines[...] = lines_of(source, planes, False)


def bring(block, planes):
    lines, depth = block.value.shape
    vmem = pl.BlockSpec(memory_space=pltpu.VMEM)
    return pl.pallas_call(
        functools.partial(bring_kernel, planes),
        out_shape=jax.ShapeDtypeStruct(
            (lines // planes, planes * depth), block.value.dtype
        ),
        in_specs=[vmem],
        out_specs=vmem,
        compiler_params=PARAMS,
        name="bring",
    )(block.value)


def local(field, even_vectors, odd_vectors):
    count = lax.axis_size("gx")
    slices = lax.axis_size("gz")
    rows, planes, depth = field.shape
    modes = even_vectors.shape[0]
    masks = [1 << b | 1 for b in range(1, count.bit_length() - 1)]

    def widen(vectors, step):
        pairs = [(i, i ^ step) for i in range(slices)]
        return jnp.concatenate((vectors, lax.ppermute(vectors, "gz", pairs)))

    def after(block, *values):
        value = lax.optimization_barrier((block.value, *values))[0]
        return Block(value, block.even, block.odd)

    vectors = jnp.stack((even_vectors, odd_vectors))[None]
    steps = [1 << b for b in range(slices.bit_length() - 1)]
    held = [Block(field.reshape(rows * planes, depth), 0, 0)]
    while masks:
        a, b = (masks + masks)[:2]
        crossed = len(masks) > 1
        near = [send(block, a, b, count) for block in held]
        far = [send(block, b, a, count) for block in held] if crossed else []
        if steps:
            vectors = widen(vectors, steps.pop(0))
            near[0] = after(near[0], vectors)
        across = [send(block, b, a, count) for block in near] if crossed else []
        held += near + far + across
        masks = masks[2:]
    for step in steps:
        vectors = widen(vectors, step)
    own_lines = bring(held[0], planes)
    others = []
    for block in held[:-1]:
        if others:
            block = after(block, others[0].value, own_lines)
        others.append(send(block, 1, 1, count))
    others.append(send(after(held[-1], vectors), 1, 1, count))

    both = held[:-1] + others[:-1] + [held[-1], others[-1]]
    pairs, left = [], list(range(len(both)))
    while left:
        i = left.pop(0)
        j = next(
            j
            for j in left
            if both[j].even == both[i].even ^ (count - 1)
            and both[j].odd == both[i].odd ^ (count - 1)
        )
        left.remove(j)
        pairs.append((j, i))
    pairs = [(both[i], both[j]) for j, i in sorted(pairs)]
    ready = [(pair[0], prepare(pair, planes)) for pair in pairs[:-2]]
    sums, matrices = combine(
        vectors, ready, pairs[-2], pairs[-1][0], count, planes
    )
    even, odd = finish(matrices, own_lines, pairs[-1][1], sums, planes)
    return even.reshape(modes, planes, depth), odd.reshape(modes, planes, depth)


def solution(mesh):
    placed = (P("gx", None, "gz"), P("gx", "gz"), P("gx", "gz"))
    return jax.shard_map(
        local,
        mesh=mesh,
        in_specs=placed,
        out_specs=(P("gx", None, "gz"), P("gx", None, "gz")),
        check_vma=False,
    )
```

```python
import functools

import jax
import jax.numpy as jnp
from jax import lax
from jax.experimental import pallas as pl
from jax.experimental.pallas import tpu as pltpu
from jax.sharding import PartitionSpec as P

PARAMS = pltpu.CompilerParams(vmem_limit_bytes=48 * 1024 * 1024)
CHUNK = 16


class Block:
    def __init__(self, value, even, odd):
        self.value, self.even, self.odd = value, even, odd

    def place(self, count):
        me = lax.axis_index("gx")
        bits = sum((me >> b) & 1 for b in range(count.bit_length() - 1))
        at = me ^ jnp.where((bits & 1) == 0, self.even, self.odd)
        upper = (at >= count // 2).astype(jnp.int32)
        block = jnp.where(upper == 1, count - 1 - at, at)
        return upper, lax.axis_index("gz") ^ block


def send(block, even, odd, count):
    pairs = [(g, g ^ (odd if g.bit_count() & 1 else even)) for g in range(count)]
    if even.bit_count() & 1:
        offsets = even ^ block.odd, odd ^ block.even
    else:
        offsets = even ^ block.even, odd ^ block.odd
    return Block(lax.ppermute(block.value, "gx", pairs), *offsets)


def parity_lines(first, second, planes, even, odd):
    lines, depth = first.shape
    rows = lines // planes
    for j in range(0, rows, CHUNK):
        evens, odds = [], []
        for i in range(j, j + CHUNK):
            a = first[pl.ds(i * planes, planes), :]
            b = second[pl.ds((rows - 1 - i) * planes, planes), :]
            evens.append(a + b)
            odds.append(a - b)
        for part, ref in ((evens, even), (odds, odd)):
            part = jnp.swapaxes(jnp.stack(part), 0, 1)
            for y in range(planes):
                ref[pl.ds(j, CHUNK), pl.ds(y * depth, depth)] = part[y]


def oriented(vectors, place):
    upper, at = place()
    modes, rows = vectors.shape[2:]
    row = lax.broadcasted_iota(jnp.int32, (rows, rows), 0)
    column = lax.broadcasted_iota(jnp.int32, (rows, rows), 1)
    chosen = jnp.where(upper == 1, rows - 1 - column, column)
    order = jnp.where(row == chosen, 1.0, 0.0).astype(vectors.dtype)
    sign = jnp.where(upper == 1, -1.0, 1.0)
    even, odd = (
        jnp.dot(vectors[at, parity], order, preferred_element_type=jnp.float32)
        for parity in (0, 1)
    )
    return even.astype(vectors.dtype), (odd * sign).astype(vectors.dtype)


def prepare_kernel(planes, first, second, even, odd):
    parity_lines(first, second, planes, even, odd)


def prepare(pair, planes):
    lines, depth = pair[0].value.shape
    shape = jax.ShapeDtypeStruct((lines // planes, planes * depth), jnp.bfloat16)
    vmem = pl.BlockSpec(memory_space=pltpu.VMEM)
    return pl.pallas_call(
        functools.partial(prepare_kernel, planes),
        out_shape=(shape, shape),
        in_specs=[vmem, vmem],
        out_specs=(vmem, vmem),
        compiler_params=PARAMS,
        name="prepare",
    )(pair[0].value, pair[1].value)


def combine_kernel(places, planes, vectors, first, second, *refs):
    *lines, sums, following, even, odd = refs
    matrices = [oriented(vectors, place) for place in places]
    for parity in (0, 1):
        following[parity] = matrices[-1][parity]
    parity_lines(first, second, planes, even, odd)
    for parity, fresh in enumerate((even, odd)):
        matrix = jnp.concatenate([both[parity] for both in matrices[:-1]], axis=1)
        parts = jnp.concatenate(
            [ref[...] for ref in lines[parity::2]] + [fresh[...]], axis=0
        )
        sums[parity] = jnp.dot(matrix, parts, preferred_element_type=jnp.float32)


def combine(vectors, ready, pair, following, count, planes):
    first, second = (block.value for block in pair)
    lines, depth = first.shape
    rows = lines // planes
    modes = vectors.shape[2]
    blocks = [block for block, _ in ready] + [pair[0], following]
    operands = [vectors, first, second] + [part for _, both in ready for part in both]
    vmem = pl.BlockSpec(memory_space=pltpu.VMEM)
    return pl.pallas_call(
        functools.partial(
            combine_kernel,
            [functools.partial(block.place, count) for block in blocks],
            planes,
        ),
        out_shape=(
            jax.ShapeDtypeStruct((2, modes, planes * depth), jnp.float32),
            jax.ShapeDtypeStruct((2, modes, rows), vectors.dtype),
        ),
        in_specs=[vmem] * len(operands),
        out_specs=(vmem, vmem),
        scratch_shapes=[pltpu.VMEM((rows, planes * depth), jnp.bfloat16)] * 2,
        compiler_params=PARAMS,
        name="combine",
    )(*operands)


def finish_kernel(planes, matrices, lines, second, sums, *outs):
    depth = second.shape[1]
    modes = matrices.shape[1]
    here = lines[...]
    there = lines_of(second, planes, True)
    for parity, parts in enumerate((here + there, here - there)):
        result = sums[parity] + jnp.dot(
            matrices[parity], parts, preferred_element_type=jnp.float32
        )
        for y in range(planes):
            outs[parity][pl.ds(y, modes, stride=planes), :] = result[
                :, y * depth : (y + 1) * depth
            ]


def finish(matrices, lines, second, sums, planes):
    depth = second.value.shape[1]
    modes = matrices.shape[1]
    shape = jax.ShapeDtypeStruct((modes * planes, depth), jnp.float32)
    vmem = pl.BlockSpec(memory_space=pltpu.VMEM)
    return pl.pallas_call(
        functools.partial(finish_kernel, planes),
        out_shape=(shape, shape),
        in_specs=[vmem] * 4,
        out_specs=(vmem, vmem),
        compiler_params=PARAMS,
        name="finish",
    )(matrices, lines, second.value, sums)


def lines_of(block, planes, backwards):
    rows = block.shape[0] // planes
    order = range(rows - 1, -1, -1) if backwards else range(rows)
    lines = jnp.stack([block[pl.ds(i * planes, planes), :] for i in order])
    lines = jnp.swapaxes(lines, 0, 1)
    return jnp.concatenate([lines[y] for y in range(planes)], axis=1)


def bring_kernel(planes, source, lines):
    lines[...] = lines_of(source, planes, False)


def bring(block, planes):
    lines, depth = block.value.shape
    vmem = pl.BlockSpec(memory_space=pltpu.VMEM)
    return pl.pallas_call(
        functools.partial(bring_kernel, planes),
        out_shape=jax.ShapeDtypeStruct(
            (lines // planes, planes * depth), block.value.dtype
        ),
        in_specs=[vmem],
        out_specs=vmem,
        compiler_params=PARAMS,
        name="bring",
    )(block.value)


def local(field, even_vectors, odd_vectors):
    count = lax.axis_size("gx")
    slices = lax.axis_size("gz")
    rows, planes, depth = field.shape
    modes = even_vectors.shape[0]
    masks = [1 << b | 1 for b in range(1, count.bit_length() - 1)]

    def widen(vectors, step):
        pairs = [(i, i ^ step) for i in range(slices)]
        return jnp.concatenate((vectors, lax.ppermute(vectors, "gz", pairs)))

    def after(block, *values):
        value = lax.optimization_barrier((block.value, *values))[0]
        return Block(value, block.even, block.odd)

    vectors = jnp.stack((even_vectors, odd_vectors))[None]
    steps = [1 << b for b in range(slices.bit_length() - 1)]
    held = [Block(field.reshape(rows * planes, depth), 0, 0)]
    while masks:
        a, b = (masks + masks)[:2]
        crossed = len(masks) > 1
        far = [send(block, b, a, count) for block in held] if crossed else []
        near = [send(block, a, b, count) for block in held]
        if steps:
            vectors = widen(vectors, steps.pop(0))
            near[0] = after(near[0], vectors)
        across = [send(block, b, a, count) for block in near] if crossed else []
        held += near + far + across
        masks = masks[2:]
    for step in steps:
        vectors = widen(vectors, step)
    own_lines = bring(held[0], planes)
    others = []
    for block in held[:-1]:
        if others:
            block = after(block, others[0].value, own_lines)
        others.append(send(block, 1, 1, count))
    others.append(send(after(held[-1], vectors), 1, 1, count))

    both = held[:-1] + others[:-1] + [held[-1], others[-1]]
    pairs, left = [], list(range(len(both)))
    while left:
        i = left.pop(0)
        j = next(
            j
            for j in left
            if both[j].even == both[i].even ^ (count - 1)
            and both[j].odd == both[i].odd ^ (count - 1)
        )
        left.remove(j)
        pairs.append((j, i))
    pairs = [(both[i], both[j]) for j, i in sorted(pairs)]
    ready = [(pair[0], prepare(pair, planes)) for pair in pairs[:-2]]
    sums, matrices = combine(
        vectors, ready, pairs[-2], pairs[-1][0], count, planes
    )
    even, odd = finish(matrices, own_lines, pairs[-1][1], sums, planes)
    return even.reshape(modes, planes, depth), odd.reshape(modes, planes, depth)


def solution(mesh):
    placed = (P("gx", None, "gz"), P("gx", "gz"), P("gx", "gz"))
    return jax.shard_map(
        local,
        mesh=mesh,
        in_specs=placed,
        out_specs=(P("gx", None, "gz"), P("gx", None, "gz")),
        check_vma=False,
    )
```

```python
import functools

import jax
import jax.numpy as jnp
from jax import lax
from jax.experimental import pallas as pl
from jax.experimental.pallas import tpu as pltpu
from jax.sharding import PartitionSpec as P

PARAMS = pltpu.CompilerParams(vmem_limit_bytes=48 * 1024 * 1024)
CHUNK = 16
GROUP = 8


class Block:
    def __init__(self, value, even, odd):
        self.value, self.even, self.odd = value, even, odd

    def place(self, count):
        me = lax.axis_index("gx")
        bits = sum((me >> b) & 1 for b in range(count.bit_length() - 1))
        at = me ^ jnp.where((bits & 1) == 0, self.even, self.odd)
        upper = (at >= count // 2).astype(jnp.int32)
        block = jnp.where(upper == 1, count - 1 - at, at)
        return upper, lax.axis_index("gz") ^ block


def send(block, even, odd, count):
    pairs = [(g, g ^ (odd if g.bit_count() & 1 else even)) for g in range(count)]
    if even.bit_count() & 1:
        offsets = even ^ block.odd, odd ^ block.even
    else:
        offsets = even ^ block.even, odd ^ block.odd
    return Block(lax.ppermute(block.value, "gx", pairs), *offsets)


def parity_lines(first, second, planes, even, odd):
    lines, depth = first.shape
    rows = lines // planes
    for j in range(0, rows, CHUNK):
        evens, odds = [], []
        for i in range(j, j + CHUNK):
            a = first[pl.ds(i * planes, planes), :]
            b = second[pl.ds((rows - 1 - i) * planes, planes), :]
            evens.append(a + b)
            odds.append(a - b)
        for part, ref in ((evens, even), (odds, odd)):
            part = jnp.swapaxes(jnp.stack(part), 0, 1)
            for y in range(planes):
                ref[pl.ds(j, CHUNK), pl.ds(y * depth, depth)] = part[y]


def oriented(vectors, place):
    upper, at = place()
    modes, rows = vectors.shape[2:]
    row = lax.broadcasted_iota(jnp.int32, (rows, rows), 0)
    column = lax.broadcasted_iota(jnp.int32, (rows, rows), 1)
    chosen = jnp.where(upper == 1, rows - 1 - column, column)
    order = jnp.where(row == chosen, 1.0, 0.0).astype(vectors.dtype)
    sign = jnp.where(upper == 1, -1.0, 1.0)
    even, odd = (
        jnp.dot(vectors[at, parity], order, preferred_element_type=jnp.float32)
        for parity in (0, 1)
    )
    return even.astype(vectors.dtype), (odd * sign).astype(vectors.dtype)


def prepare_kernel(planes, first, second, even, odd):
    parity_lines(first, second, planes, even, odd)


def prepare(pair, planes):
    lines, depth = pair[0].value.shape
    shape = jax.ShapeDtypeStruct((lines // planes, planes * depth), jnp.bfloat16)
    vmem = pl.BlockSpec(memory_space=pltpu.VMEM)
    return pl.pallas_call(
        functools.partial(prepare_kernel, planes),
        out_shape=(shape, shape),
        in_specs=[vmem, vmem],
        out_specs=(vmem, vmem),
        compiler_params=PARAMS,
        name="prepare",
    )(pair[0].value, pair[1].value)


def combine_kernel(places, planes, vectors, first, second, *refs):
    *lines, sums, following, even, odd = refs
    matrices = [oriented(vectors, place) for place in places]
    for parity in (0, 1):
        following[parity] = matrices[-1][parity]
    parity_lines(first, second, planes, even, odd)
    for parity, fresh in enumerate((even, odd)):
        matrix = jnp.concatenate([both[parity] for both in matrices[:-1]], axis=1)
        parts = jnp.concatenate(
            [ref[...] for ref in lines[parity::2]] + [fresh[...]], axis=0
        )
        sums[parity] = jnp.dot(matrix, parts, preferred_element_type=jnp.float32)


def combine(vectors, ready, pair, following, count, planes):
    first, second = (block.value for block in pair)
    lines, depth = first.shape
    rows = lines // planes
    modes = vectors.shape[2]
    blocks = [block for block, _ in ready] + [pair[0], following]
    operands = [vectors, first, second] + [part for _, both in ready for part in both]
    vmem = pl.BlockSpec(memory_space=pltpu.VMEM)
    return pl.pallas_call(
        functools.partial(
            combine_kernel,
            [functools.partial(block.place, count) for block in blocks],
            planes,
        ),
        out_shape=(
            jax.ShapeDtypeStruct((2, modes, planes * depth), jnp.float32),
            jax.ShapeDtypeStruct((2, modes, rows), vectors.dtype),
        ),
        in_specs=[vmem] * len(operands),
        out_specs=(vmem, vmem),
        scratch_shapes=[pltpu.VMEM((rows, planes * depth), jnp.bfloat16)] * 2,
        compiler_params=PARAMS,
        name="combine",
    )(*operands)


def finish_kernel(planes, matrices, lines, second, sums, *outs):
    depth = second.shape[1]
    modes = matrices.shape[1]
    rows = second.shape[0] // planes
    there = jnp.swapaxes(
        jnp.stack(
            [second[pl.ds(i * planes, planes), :] for i in reversed(range(rows))]
        ),
        0,
        1,
    )
    for start in range(0, planes, GROUP):
        columns = pl.ds(start * depth, GROUP * depth)
        here = lines[:, columns]
        other = jnp.concatenate([there[y] for y in range(start, start + GROUP)], axis=1)
        for parity, parts in enumerate((here + other, here - other)):
            result = sums[parity, :, columns] + jnp.dot(
                matrices[parity], parts, preferred_element_type=jnp.float32
            )
            for y in range(GROUP):
                outs[parity][pl.ds(start + y, modes, stride=planes), :] = result[
                    :, y * depth : (y + 1) * depth
                ]


def finish(matrices, lines, second, sums, planes):
    depth = second.value.shape[1]
    modes = matrices.shape[1]
    shape = jax.ShapeDtypeStruct((modes * planes, depth), jnp.float32)
    vmem = pl.BlockSpec(memory_space=pltpu.VMEM)
    return pl.pallas_call(
        functools.partial(finish_kernel, planes),
        out_shape=(shape, shape),
        in_specs=[vmem] * 4,
        out_specs=(vmem, vmem),
        compiler_params=PARAMS,
        name="finish",
    )(matrices, lines, second.value, sums)


def lines_of(block, planes, backwards):
    rows = block.shape[0] // planes
    order = range(rows - 1, -1, -1) if backwards else range(rows)
    lines = jnp.stack([block[pl.ds(i * planes, planes), :] for i in order])
    lines = jnp.swapaxes(lines, 0, 1)
    return jnp.concatenate([lines[y] for y in range(planes)], axis=1)


def bring_kernel(planes, source, lines):
    lines[...] = lines_of(source, planes, False)


def bring(block, planes):
    lines, depth = block.value.shape
    vmem = pl.BlockSpec(memory_space=pltpu.VMEM)
    return pl.pallas_call(
        functools.partial(bring_kernel, planes),
        out_shape=jax.ShapeDtypeStruct(
            (lines // planes, planes * depth), block.value.dtype
        ),
        in_specs=[vmem],
        out_specs=vmem,
        compiler_params=PARAMS,
        name="bring",
    )(block.value)


def local(field, even_vectors, odd_vectors):
    count = lax.axis_size("gx")
    slices = lax.axis_size("gz")
    rows, planes, depth = field.shape
    modes = even_vectors.shape[0]
    masks = [1 << b | 1 for b in range(1, count.bit_length() - 1)]

    def widen(vectors, step):
        pairs = [(i, i ^ step) for i in range(slices)]
        return jnp.concatenate((vectors, lax.ppermute(vectors, "gz", pairs)))

    def after(block, *values):
        value = lax.optimization_barrier((block.value, *values))[0]
        return Block(value, block.even, block.odd)

    vectors = jnp.stack((even_vectors, odd_vectors))[None]
    steps = [1 << b for b in range(slices.bit_length() - 1)]
    held = [Block(field.reshape(rows * planes, depth), 0, 0)]
    while masks:
        a, b = (masks + masks)[:2]
        crossed = len(masks) > 1
        far = [send(block, b, a, count) for block in held] if crossed else []
        near = [send(block, a, b, count) for block in held]
        if steps:
            vectors = widen(vectors, steps.pop(0))
            near[0] = after(near[0], vectors)
        across = [send(block, b, a, count) for block in near] if crossed else []
        held += near + far + across
        masks = masks[2:]
    for step in steps:
        vectors = widen(vectors, step)
    own_lines = bring(held[0], planes)
    others = []
    for block in held[:-1]:
        if others:
            block = after(block, others[0].value, own_lines)
        others.append(send(block, 1, 1, count))
    others.append(send(after(held[-1], vectors), 1, 1, count))

    both = held[:-1] + others[:-1] + [held[-1], others[-1]]
    pairs, left = [], list(range(len(both)))
    while left:
        i = left.pop(0)
        j = next(
            j
            for j in left
            if both[j].even == both[i].even ^ (count - 1)
            and both[j].odd == both[i].odd ^ (count - 1)
        )
        left.remove(j)
        pairs.append((j, i))
    pairs = [(both[i], both[j]) for j, i in sorted(pairs)]
    ready = [(pair[0], prepare(pair, planes)) for pair in pairs[:-2]]
    sums, matrices = combine(
        vectors, ready, pairs[-2], pairs[-1][0], count, planes
    )
    even, odd = finish(matrices, own_lines, pairs[-1][1], sums, planes)
    return even.reshape(modes, planes, depth), odd.reshape(modes, planes, depth)


def solution(mesh):
    placed = (P("gx", None, "gz"), P("gx", "gz"), P("gx", "gz"))
    return jax.shard_map(
        local,
        mesh=mesh,
        in_specs=placed,
        out_specs=(P("gx", None, "gz"), P("gx", None, "gz")),
        check_vma=False,
    )
```

```python
import functools

import jax
import jax.numpy as jnp
from jax import lax
from jax.experimental import pallas as pl
from jax.experimental.pallas import tpu as pltpu
from jax.sharding import PartitionSpec as P

PARAMS = pltpu.CompilerParams(vmem_limit_bytes=48 * 1024 * 1024)
CHUNK = 32


class Block:
    def __init__(self, value, even, odd):
        self.value, self.even, self.odd = value, even, odd

    def place(self, count):
        me = lax.axis_index("gx")
        bits = sum((me >> b) & 1 for b in range(count.bit_length() - 1))
        at = me ^ jnp.where((bits & 1) == 0, self.even, self.odd)
        upper = (at >= count // 2).astype(jnp.int32)
        block = jnp.where(upper == 1, count - 1 - at, at)
        return upper, lax.axis_index("gz") ^ block


def send(block, even, odd, count):
    pairs = [(g, g ^ (odd if g.bit_count() & 1 else even)) for g in range(count)]
    if even.bit_count() & 1:
        offsets = even ^ block.odd, odd ^ block.even
    else:
        offsets = even ^ block.even, odd ^ block.odd
    return Block(lax.ppermute(block.value, "gx", pairs), *offsets)


def parity_lines(first, second, planes, even, odd):
    lines, depth = first.shape
    rows = lines // planes
    for j in range(0, rows, CHUNK):
        evens, odds = [], []
        for i in range(j, j + CHUNK):
            a = first[pl.ds(i * planes, planes), :]
            b = second[pl.ds((rows - 1 - i) * planes, planes), :]
            evens.append(a + b)
            odds.append(a - b)
        for part, ref in ((evens, even), (odds, odd)):
            part = jnp.swapaxes(jnp.stack(part), 0, 1)
            for y in range(planes):
                ref[pl.ds(j, CHUNK), pl.ds(y * depth, depth)] = part[y]


def oriented(vectors, place):
    upper, at = place()
    modes, rows = vectors.shape[2:]
    row = lax.broadcasted_iota(jnp.int32, (rows, rows), 0)
    column = lax.broadcasted_iota(jnp.int32, (rows, rows), 1)
    chosen = jnp.where(upper == 1, rows - 1 - column, column)
    order = jnp.where(row == chosen, 1.0, 0.0).astype(vectors.dtype)
    sign = jnp.where(upper == 1, -1.0, 1.0)
    even, odd = (
        jnp.dot(vectors[at, parity], order, preferred_element_type=jnp.float32)
        for parity in (0, 1)
    )
    return even.astype(vectors.dtype), (odd * sign).astype(vectors.dtype)


def prepare_kernel(planes, first, second, even, odd):
    parity_lines(first, second, planes, even, odd)


def prepare(pair, planes):
    lines, depth = pair[0].value.shape
    shape = jax.ShapeDtypeStruct((lines // planes, planes * depth), jnp.bfloat16)
    vmem = pl.BlockSpec(memory_space=pltpu.VMEM)
    return pl.pallas_call(
        functools.partial(prepare_kernel, planes),
        out_shape=(shape, shape),
        in_specs=[vmem, vmem],
        out_specs=(vmem, vmem),
        compiler_params=PARAMS,
        name="prepare",
    )(pair[0].value, pair[1].value)


def combine_kernel(places, planes, vectors, first, second, *refs):
    *lines, sums, following, even, odd = refs
    matrices = [oriented(vectors, place) for place in places]
    for parity in (0, 1):
        following[parity] = matrices[-1][parity]
    parity_lines(first, second, planes, even, odd)
    for parity, fresh in enumerate((even, odd)):
        matrix = jnp.concatenate([both[parity] for both in matrices[:-1]], axis=1)
        parts = jnp.concatenate(
            [ref[...] for ref in lines[parity::2]] + [fresh[...]], axis=0
        )
        sums[parity] = jnp.dot(matrix, parts, preferred_element_type=jnp.float32)


def combine(vectors, ready, pair, following, count, planes):
    first, second = (block.value for block in pair)
    lines, depth = first.shape
    rows = lines // planes
    modes = vectors.shape[2]
    blocks = [block for block, _ in ready] + [pair[0], following]
    operands = [vectors, first, second] + [part for _, both in ready for part in both]
    vmem = pl.BlockSpec(memory_space=pltpu.VMEM)
    return pl.pallas_call(
        functools.partial(
            combine_kernel,
            [functools.partial(block.place, count) for block in blocks],
            planes,
        ),
        out_shape=(
            jax.ShapeDtypeStruct((2, modes, planes * depth), jnp.float32),
            jax.ShapeDtypeStruct((2, modes, rows), vectors.dtype),
        ),
        in_specs=[vmem] * len(operands),
        out_specs=(vmem, vmem),
        scratch_shapes=[pltpu.VMEM((rows, planes * depth), jnp.bfloat16)] * 2,
        compiler_params=PARAMS,
        name="combine",
    )(*operands)


def finish_kernel(planes, matrices, lines, second, sums, *outs):
    depth = second.shape[1]
    modes = matrices.shape[1]
    here = lines[...]
    there = lines_of(second, planes, True)
    for parity, parts in enumerate((here + there, here - there)):
        result = sums[parity] + jnp.dot(
            matrices[parity], parts, preferred_element_type=jnp.float32
        )
        for y in range(planes):
            outs[parity][pl.ds(y, modes, stride=planes), :] = result[
                :, y * depth : (y + 1) * depth
            ]


def finish(matrices, lines, second, sums, planes):
    depth = second.value.shape[1]
    modes = matrices.shape[1]
    shape = jax.ShapeDtypeStruct((modes * planes, depth), jnp.float32)
    vmem = pl.BlockSpec(memory_space=pltpu.VMEM)
    return pl.pallas_call(
        functools.partial(finish_kernel, planes),
        out_shape=(shape, shape),
        in_specs=[vmem] * 4,
        out_specs=(vmem, vmem),
        compiler_params=PARAMS,
        name="finish",
    )(matrices, lines, second.value, sums)


def lines_of(block, planes, backwards):
    rows = block.shape[0] // planes
    order = range(rows - 1, -1, -1) if backwards else range(rows)
    lines = jnp.stack([block[pl.ds(i * planes, planes), :] for i in order])
    lines = jnp.swapaxes(lines, 0, 1)
    return jnp.concatenate([lines[y] for y in range(planes)], axis=1)


def bring_kernel(planes, source, lines):
    lines[...] = lines_of(source, planes, False)


def bring(block, planes):
    lines, depth = block.value.shape
    vmem = pl.BlockSpec(memory_space=pltpu.VMEM)
    return pl.pallas_call(
        functools.partial(bring_kernel, planes),
        out_shape=jax.ShapeDtypeStruct(
            (lines // planes, planes * depth), block.value.dtype
        ),
        in_specs=[vmem],
        out_specs=vmem,
        compiler_params=PARAMS,
        name="bring",
    )(block.value)


def local(field, even_vectors, odd_vectors):
    count = lax.axis_size("gx")
    slices = lax.axis_size("gz")
    rows, planes, depth = field.shape
    modes = even_vectors.shape[0]
    masks = [1 << b | 1 for b in range(1, count.bit_length() - 1)]

    def widen(vectors, step):
        pairs = [(i, i ^ step) for i in range(slices)]
        return jnp.concatenate((vectors, lax.ppermute(vectors, "gz", pairs)))

    def after(block, *values):
        value = lax.optimization_barrier((block.value, *values))[0]
        return Block(value, block.even, block.odd)

    vectors = jnp.stack((even_vectors, odd_vectors))[None]
    steps = [1 << b for b in range(slices.bit_length() - 1)]
    held = [Block(field.reshape(rows * planes, depth), 0, 0)]
    while masks:
        a, b = (masks + masks)[:2]
        crossed = len(masks) > 1
        far = [send(block, b, a, count) for block in held] if crossed else []
        near = [send(block, a, b, count) for block in held]
        if steps:
            vectors = widen(vectors, steps.pop(0))
            near[0] = after(near[0], vectors)
        across = [send(block, b, a, count) for block in near] if crossed else []
        held += near + far + across
        masks = masks[2:]
    for step in steps:
        vectors = widen(vectors, step)
    own_lines = bring(held[0], planes)
    others = []
    for block in held[:-1]:
        if others:
            block = after(block, others[0].value, own_lines)
        others.append(send(block, 1, 1, count))
    others.append(send(after(held[-1], vectors), 1, 1, count))

    both = held[:-1] + others[:-1] + [held[-1], others[-1]]
    pairs, left = [], list(range(len(both)))
    while left:
        i = left.pop(0)
        j = next(
            j
            for j in left
            if both[j].even == both[i].even ^ (count - 1)
            and both[j].odd == both[i].odd ^ (count - 1)
        )
        left.remove(j)
        pairs.append((j, i))
    pairs = [(both[i], both[j]) for j, i in sorted(pairs)]
    ready = [(pair[0], prepare(pair, planes)) for pair in pairs[:-2]]
    sums, matrices = combine(
        vectors, ready, pairs[-2], pairs[-1][0], count, planes
    )
    even, odd = finish(matrices, own_lines, pairs[-1][1], sums, planes)
    return even.reshape(modes, planes, depth), odd.reshape(modes, planes, depth)


def solution(mesh):
    placed = (P("gx", None, "gz"), P("gx", "gz"), P("gx", "gz"))
    return jax.shard_map(
        local,
        mesh=mesh,
        in_specs=placed,
        out_specs=(P("gx", None, "gz"), P("gx", None, "gz")),
        check_vma=False,
    )
```
